32 devices in a mesh: grp: 2 (over y), bin: 4 (over z), blk: 2 (over x), sub: 2 (over core).
Axes of the slice: x: 2, y: 2, z: 4, core: 2. Of those that a mesh axis runs over, the one named last changes fastest.
Arguments:
- band: float32 [16, 8, 256, 256], P(('grp', 'bin', 'blk'), None, None, 'sub'), parts along dimension 0, as said below
- far_tiles: float32 [256, 256, 256], P(('grp', 'bin', 'blk'), None, 'sub'), parts along dimension 0, as said below
- far_list: int32 [256, 2], P(('grp', 'bin', 'blk')), parts along dimension 0, may hold values from 0 to 7, as said below
- far_count: int32 [16], P(('grp', 'bin', 'blk')), parts along dimension 0, may hold values from 1 to 16, as said below
- masked: int32 [256], P(('grp', 'bin')), parts along dimension 0, may hold values from 0 to 2047, as said below
Outputs:
- bias: float32 [4096], P(('grp', 'bin', 'blk')), parts along dimension 0
- coverage: float32 [4096], P(('grp', 'bin', 'blk')), parts along dimension 0
The draws below stay inside these ranges and needn't reach their ends.
There are 2 independent parts, one for each index of `grp`. The reference program is written for one: setup_inputs(seed, part) draws one part's arguments, and reference() takes and returns one part's arrays. A program takes and returns all parts, laid end to end along the dimension named above; each array names one. Nothing has to cross between parts.
Inputs may be any that keep to these rules, and one draw needn't show every extreme that they name: Every value is positive; each diagonal block band[r, 0] is symmetric up to rounding. `far_tiles`: every value is positive. `far_list`: column 0 is a far block's row block, held by the device that stores the slot: device d along bin and blk holds row blocks 1 * d to 1 * d + 1 - 1. Column 1 is its column block, held by another device. Of the 16 slots of one device, used or not, exactly 4 have column blocks held by each of 4 other devices. The first far_count[d] slots of device d are used; some device uses all 16. `masked`: the entries of index g of bin are distinct bins of g * 512 to g * 512 + 511.
All inputs are finite; a program needn't handle non-finite values.
Results may differ from the reference program's by a relative error of at most 0.0001.
Values sent between devices are 32-bit elements; how exact they have to be, the bound alone decides.
A program may use at most 64 MiB of HBM per device.

```python
import jax
import jax.numpy as jnp
from jax import lax

BLOCK = 256
BAND = 8
ROWS_DEV = 1
ITERS = 2
CAP = 4
FAR_DEST = 4
MASK_DEV = 32
FAR_SLOTS = 16
OWNERS = 8
BIN_GROUPS = 4
NRB = 8
NBINS = 2048
OWNER_BINS = 512


def mappability(key):
    key = jax.random.fold_in(key, 101)
    level = jax.random.uniform(key, (NBINS,), jnp.float32)
    return jnp.exp(jnp.log(0.25) + level * jnp.log(16.0)).reshape(NRB, BLOCK)


def far_layout(key):
    key = jax.random.fold_in(key, 202)
    first, second, third = jax.random.split(key, 3)
    scores = jax.random.randint(first, (OWNERS, OWNERS - 1), 0, 1 << 12) * (OWNERS - 1)
    scores = scores + jnp.arange(OWNERS - 1, dtype=jnp.int32)[None, :]
    offsets = jnp.argsort(scores, axis=1)[:, :FAR_DEST].astype(jnp.int32)
    holder = jnp.arange(OWNERS, dtype=jnp.int32)[:, None]
    target = jnp.repeat((holder + 1 + offsets) % OWNERS, CAP, axis=1)
    column = target * ROWS_DEV + jax.random.randint(second, (OWNERS, FAR_SLOTS), 0, ROWS_DEV)
    row = holder * ROWS_DEV + jax.random.randint(third, (OWNERS, FAR_SLOTS), 0, ROWS_DEV)
    return (row.reshape(-1).astype(jnp.int32), column.reshape(-1).astype(jnp.int32))


def draw_band(key, part):
    weights = mappability(key)
    key = jax.random.fold_in(key, 303)
    level = jax.random.uniform(key, (NRB, BAND, BLOCK, BLOCK), jnp.float32)
    diagonal = level[:, 0]
    level = level.at[:, 0].set(0.5 * (diagonal + jnp.swapaxes(diagonal, 1, 2)))
    factor = jnp.exp(jnp.log(0.3) + level * jnp.log(10.0))
    slope = 2.0
    padded = jnp.concatenate([weights, jnp.ones((BAND, BLOCK), jnp.float32)], axis=0)
    partner = jnp.stack([padded[offset:offset + NRB] for offset in range(BAND)], axis=1)
    distance = jnp.arange(BAND, dtype=jnp.float32)[:, None, None] * BLOCK + jnp.arange(BLOCK, dtype=jnp.float32)[None, None, :] - jnp.arange(BLOCK, dtype=jnp.float32)[None, :, None]
    decay = 1.0 / (1.0 + jnp.abs(distance) / BLOCK)
    ramp = 1.0 + slope * jnp.arange(NRB, dtype=jnp.float32) / NRB
    value = factor * (weights * ramp[:, None])[:, None, :, None] * partner[:, :, None, :] * decay[None] / 1024.0
    return value.astype(jnp.float32)


def draw_far_tiles(key, part):
    row, column = far_layout(key)
    weights = mappability(key)
    key = jax.random.fold_in(key, 404)
    level = jax.random.uniform(key, (OWNERS * FAR_SLOTS, BLOCK, BLOCK), jnp.float32)
    factor = jnp.exp(jnp.log(0.3) + level * jnp.log(10.0))
    slope = 2.0
    ramp = 1.0 + slope * row.astype(jnp.float32) / NRB
    value = factor * (weights[row] * ramp[:, None])[:, :, None] * weights[column][:, None, :] / 1024.0
    return value.astype(jnp.float32)


def draw_far_list(key, part):
    row, column = far_layout(key)
    return jnp.stack([row, column], axis=1).astype(jnp.int32)


def draw_far_count(key, part):
    key = jax.random.fold_in(key, 505)
    first, second, third = jax.random.split(key, 3)
    left_count = jax.random.randint(first, (OWNERS,), 1, FAR_SLOTS + 1)
    right_count = jax.random.randint(second, (OWNERS,), 1, FAR_SLOTS + 1)
    counted = jnp.minimum(left_count, right_count)
    busiest = jax.random.randint(third, (), 0, OWNERS)
    counted = jnp.where(jnp.arange(OWNERS, dtype=jnp.int32) == busiest, FAR_SLOTS, counted)
    return counted.astype(jnp.int32)


def draw_masked(key, part):
    key = jax.random.fold_in(key, 606)
    scores = jax.random.randint(key, (BIN_GROUPS, OWNER_BINS), 0, 1 << 10) * OWNER_BINS
    scores = scores + jnp.arange(OWNER_BINS, dtype=jnp.int32)[None, :]
    chosen = jnp.argsort(scores, axis=1)[:, :MASK_DEV].astype(jnp.int32)
    chosen = chosen + jnp.arange(BIN_GROUPS, dtype=jnp.int32)[:, None] * OWNER_BINS
    return chosen.reshape(-1).astype(jnp.int32)


def setup_inputs(seed: int = 0, part: int = 0) -> dict:
    key_list = jax.random.split(jax.random.key(seed), 6)
    part_splits = jax.random.split(jax.random.fold_in(key_list[5], part), 6)
    band = draw_band(jax.random.fold_in(jax.random.fold_in(key_list[5], part), 71), part)
    far_tiles = draw_far_tiles(jax.random.fold_in(jax.random.fold_in(key_list[5], part), 71), part)
    far_list = draw_far_list(jax.random.fold_in(jax.random.fold_in(key_list[5], part), 71), part)
    far_count = draw_far_count(jax.random.fold_in(jax.random.fold_in(key_list[5], part), 71), part)
    masked = draw_masked(jax.random.fold_in(jax.random.fold_in(key_list[5], part), 71), part)
    return {"band": band, "far_tiles": far_tiles, "far_list": far_list, "far_count": far_count, "masked": masked}


def row_sums(band, far_tiles, far_list, used, bias):
    blocks = bias.reshape(NRB, BLOCK)
    padded = jnp.concatenate([blocks, jnp.zeros((BAND, BLOCK), jnp.float32)], axis=0)
    total = jnp.zeros((NRB + BAND, BLOCK), jnp.float32)
    for offset in range(BAND):
        tiles = band[:, offset]
        forward = jnp.einsum('rij,rj->ri', tiles, padded[offset:offset + NRB], precision=lax.Precision.HIGHEST)
        total = total.at[:NRB].add(forward)
        if offset > 0:
            mirrored = jnp.einsum('rij,ri->rj', tiles, blocks, precision=lax.Precision.HIGHEST)
            total = total.at[offset:offset + NRB].add(mirrored)
    far_rows = far_list[:, 0]
    far_cols = far_list[:, 1]
    forward = used[:, None] * jnp.einsum('kij,kj->ki', far_tiles, blocks[far_cols], precision=lax.Precision.HIGHEST)
    mirrored = used[:, None] * jnp.einsum('kij,ki->kj', far_tiles, blocks[far_rows], precision=lax.Precision.HIGHEST)
    total = total.at[far_rows].add(forward)
    total = total.at[far_cols].add(mirrored)
    return total[:NRB].reshape(-1)

def reference(band, far_tiles, far_list, far_count, masked):
    keep = jnp.ones((NBINS,), jnp.float32).at[masked].set(0.0)
    valid_bins = NBINS - masked.shape[0]
    slot_index = jnp.arange(OWNERS * FAR_SLOTS, dtype=jnp.int32)
    used = (slot_index % FAR_SLOTS < jnp.repeat(far_count, FAR_SLOTS)).astype(jnp.float32)
    bias = keep
    coverage = keep
    for step in range(ITERS):
        sums = row_sums(band, far_tiles, far_list, used, bias)
        coverage = bias * sums
        mean = jnp.sum(coverage) / valid_bins
        bias = jnp.sqrt(bias * mean / sums)
    return (bias, coverage)
```

```python
import functools

import jax
import jax.numpy as jnp
from jax import lax
from jax.experimental import pallas as pl
from jax.experimental.pallas import tpu as pltpu
from jax.sharding import PartitionSpec as P

MESH = pl.DeviceIdType.MESH
LANES = 128
GROUP = 32


def each(count, body):
    if count <= 16:
        for index in range(count):
            body(index)
    else:
        lax.fori_loop(0, count, lambda index, carry: (body(index), carry)[1], 0)


def landed(window, sem):
    pltpu.make_async_copy(window, window, sem).wait()


def to_column(row):
    parts = []
    for start in range(0, row.shape[1], LANES):
        piece = jnp.broadcast_to(row[:, start:start + LANES], (LANES, LANES))
        parts.append(jnp.transpose(piece))
    return jnp.concatenate(parts, axis=0)


def kernel(owners, blks, reach, slots, valid, masked, far_list, far_count, band, far_tiles,
           bias_out, cov_out, tiles, column, rows, bias_send, bias_first, bias_second, mirror_send, mirror_all,
           half_send, half_recv, total_send, total_all, load_sem, bias_sem, mirror_sem,
           half_sem, total_sem):
    bias_all = (bias_first, bias_second)
    height = column.shape[0]
    count = reach + slots
    device = lax.axis_index("bin") * blks + lax.axis_index("blk")
    side = lax.axis_index("sub")

    def place(owner, core):
        return {"bin": owner // blks, "blk": lax.rem(owner, blks), "sub": core}

    def other(index):
        return lax.rem(device + 1 + index, owners)

    loads = [pltpu.make_async_copy(band.at[0], tiles.at[pl.ds(0, reach)], load_sem.at[0])]
    half_slots = slots // 2
    for piece in range(2):
        loads.append(pltpu.make_async_copy(
            far_tiles.at[pl.ds(piece * half_slots, half_slots)],
            tiles.at[pl.ds(reach + piece * half_slots, half_slots)],
            load_sem.at[1 + piece],
        ))
    for load in loads:
        load.start()
    chunks = [(0, reach), (reach, reach + half_slots), (reach + half_slots, count)]

    barrier = pltpu.get_barrier_semaphore()

    def greet(index):
        pl.semaphore_signal(barrier, inc=1, device_id=place(other(index), side), device_id_type=MESH)

    def greet_across(index):
        pl.semaphore_signal(barrier, inc=1, device_id=place(index, 1 - side), device_id_type=MESH)

    each(owners - 1, greet)
    each(owners, greet_across)

    bins = device * height + lax.broadcasted_iota(jnp.int32, (1, height), 1)
    hit = bins == masked[0]
    for index in range(1, masked.shape[0]):
        hit = jnp.logical_or(hit, bins == masked[index])
    keep = jnp.where(hit, 0.0, 1.0).astype(jnp.float32)

    def own_half(row):
        return jnp.where(side == 0, row[:, :LANES], row[:, LANES:])

    for step in range(2):
        bias_all[step][pl.ds(owners, reach), :] = jnp.zeros((reach, LANES), jnp.float32)
        mirror_all[step, pl.ds(device, 1), :] = jnp.zeros((1, LANES), jnp.float32)

    def send_bias(step, row):
        half = own_half(row)
        bias_send[step] = half
        bias_all[step][pl.ds(device, 1), :] = half

        def send(index):
            pltpu.make_async_remote_copy(
                src_ref=bias_send.at[step],
                dst_ref=bias_all[step].at[pl.ds(device, 1)],
                send_sem=bias_sem.at[0, step],
                recv_sem=bias_sem.at[1, step],
                device_id=place(other(index), side),
                device_id_type=MESH,
            ).start()

        each(owners - 1, send)

    used = [index < far_count[0] for index in range(slots)]

    def mirror(step, wait):
        sums = []
        for number, (first, last) in enumerate(chunks):
            if wait:
                loads[number].wait()
            first_tile = max(first, 1)

            def body(index, held):
                window = pl.ds(pl.multiple_of(index * GROUP, GROUP), GROUP)
                own = column[window, :]
                return tuple(
                    old + jnp.sum((tiles[first_tile + at, window, :] * own).reshape(GROUP // 8, 8, LANES), axis=0)
                    for at, old in enumerate(held)
                )

            zero = jnp.zeros((8, LANES), jnp.float32)
            sums.extend(lax.fori_loop(0, height // GROUP, body, (zero,) * (last - first_tile)))
        holder = lax.broadcasted_iota(jnp.int32, (owners, LANES), 0)
        placed = jnp.zeros((owners, LANES), jnp.float32)
        for at, partial in enumerate(sums):
            tile = at + 1
            if tile < reach:
                target = device + tile
            else:
                slot = tile - reach
                target = jnp.where(used[slot], far_list[slot, 1], -1)
            total = jnp.sum(partial, axis=0, keepdims=True)
            placed = placed + jnp.where(holder == target, total, 0.0)
        mirror_send[step] = placed

    def send_mirror(step):
        def send(index):
            owner = other(index)
            pltpu.make_async_remote_copy(
                src_ref=mirror_send.at[step, pl.ds(owner, 1)],
                dst_ref=mirror_all.at[step, pl.ds(device, 1)],
                send_sem=mirror_sem.at[0, step],
                recv_sem=mirror_sem.at[1, step],
                device_id=place(owner, side),
                device_id_type=MESH,
            ).start()

        each(owners - 1, send)

    def forward(step):
        landed(bias_all[step].at[pl.ds(0, owners - 1)], bias_sem.at[1, step])
        factors = []
        for tile in range(count):
            if tile < reach:
                factor = bias_all[step][pl.ds(device + tile, 1), :]
            else:
                slot = tile - reach
                factor = bias_all[step][pl.ds(far_list[slot, 1], 1), :]
                factor = jnp.where(used[slot], factor, 0.0)
            factors.append(jnp.broadcast_to(factor, (8, LANES))[None])

        def body(index, form):
            window = pl.ds(pl.multiple_of(index * GROUP, GROUP), GROUP)

            def term(tile):
                return tiles[tile, window, :].reshape(GROUP // 8, 8, LANES) * factors[tile]

            near = term(0)
            far = term(1)
            for tile in range(2, count):
                far = far + term(tile)
            whole = near + far
            rows[window, :] = whole.reshape(GROUP, LANES)
            if step == 0:
                return form
            own = column[window, :].reshape(GROUP // 8, 8, LANES)
            return form + jnp.sum(own * (whole + far), axis=0)

        form = lax.fori_loop(0, height // GROUP, body, jnp.zeros((8, LANES), jnp.float32))
        pieces = []
        for start in range(0, height, LANES):
            piece = jnp.transpose(rows[pl.ds(start, LANES), :])
            pieces.append(jnp.sum(piece, axis=0, keepdims=True))
        return jnp.concatenate(pieces, axis=1), jnp.sum(form, axis=0, keepdims=True)

    def join(step, row_part):
        landed(mirror_all.at[step, pl.ds(0, owners - 1)], mirror_sem.at[1, step])
        col_half = jnp.sum(mirror_all[step], axis=0, keepdims=True)
        empty = jnp.zeros_like(col_half)
        part = row_part + jnp.concatenate(
            [jnp.where(side == 0, col_half, empty), jnp.where(side == 0, empty, col_half)], axis=1
        )
        half_send[step] = part
        copy = pltpu.make_async_remote_copy(
            src_ref=half_send.at[step],
            dst_ref=half_recv.at[step],
            send_sem=half_sem.at[0, step],
            recv_sem=half_sem.at[1, step],
            device_id=place(device, 1 - side),
            device_id_type=MESH,
        )
        copy.start()
        copy.wait_recv()
        return part + half_recv[step]

    column[...] = to_column(keep)
    pl.semaphore_wait(barrier, 2 * owners - 1)
    send_bias(0, keep)
    mirror(0, True)
    send_mirror(0)
    row_part, _ = forward(0)
    sums = join(0, row_part)

    scaled = keep / jnp.sqrt(sums)
    send_bias(1, scaled)
    column[...] = to_column(scaled)
    mirror(1, False)
    send_mirror(1)
    row_part, form = forward(1)

    packet = jnp.concatenate([own_half(keep * sums), form], axis=0)
    total_send[...] = packet
    total_all[device * 2 + side] = packet

    def send_total(owner, core):
        pltpu.make_async_remote_copy(
            src_ref=total_send,
            dst_ref=total_all.at[device * 2 + side],
            send_sem=total_sem.at[0],
            recv_sem=total_sem.at[1],
            device_id=place(owner, core),
            device_id_type=MESH,
        ).start()

    each(owners - 1, lambda index: send_total(other(index), side))
    each(owners, lambda index: send_total(index, 1 - side))
    product = join(1, row_part)
    landed(total_all.at[pl.ds(0, 2 * owners - 1)], total_sem.at[1])
    totals = jnp.sum(jnp.sum(total_all[...], axis=0), axis=1, keepdims=True) / valid
    first = totals[0:1]
    mean = first * totals[1:2]
    bias_out[...] = jnp.sqrt(scaled * mean / product)
    cov_out[...] = scaled * product * first

    for step in range(2):
        landed(bias_all[step].at[pl.ds(0, owners - 1)], bias_sem.at[0, step])
        landed(mirror_all.at[step, pl.ds(0, owners - 1)], mirror_sem.at[0, step])
        landed(half_send.at[step], half_sem.at[0, step])
    landed(total_all.at[pl.ds(0, 2 * owners - 1)], total_sem.at[0])


def local(band, far_tiles, far_list, far_count, masked):
    reach, block, half = band.shape[1:]
    slots = far_tiles.shape[0]
    owners = lax.axis_size(("bin", "blk"))
    valid = owners * block - lax.axis_size("bin") * masked.shape[0]
    smem = pl.BlockSpec(memory_space=pltpu.SMEM)
    hbm = pl.BlockSpec(memory_space=pl.ANY)
    vmem = pl.BlockSpec(memory_space=pltpu.VMEM)
    f32 = jnp.float32
    dma = pltpu.SemaphoreType.DMA
    bias, coverage = pl.pallas_call(
        functools.partial(kernel, owners, lax.axis_size("blk"), reach, slots, float(valid)),
        out_shape=(jax.ShapeDtypeStruct((1, block), f32), jax.ShapeDtypeStruct((1, block), f32)),
        in_specs=[smem, smem, smem, hbm, hbm],
        out_specs=(vmem, vmem),
        scratch_shapes=[
            pltpu.VMEM((reach + slots, block, half), f32),
            pltpu.VMEM((block, half), f32),
            pltpu.VMEM((block, half), f32),
            pltpu.VMEM((2, 1, half), f32),
            pltpu.VMEM((owners + reach, half), f32),
            pltpu.VMEM((owners + reach, half), f32),
            pltpu.VMEM((2, owners, half), f32),
            pltpu.VMEM((2, owners, half), f32),
            pltpu.VMEM((2, 1, block), f32),
            pltpu.VMEM((2, 1, block), f32),
            pltpu.VMEM((2, half), f32),
            pltpu.VMEM((2 * owners, 2, half), f32),
            dma((3,)),
            dma((2, 2)),
            dma((2, 2)),
            dma((2, 2)),
            dma((2,)),
        ],
        compiler_params=pltpu.CompilerParams(collective_id=0, has_side_effects=True),
    )(masked, far_list, far_count, band, far_tiles)
    return bias.reshape(-1), coverage.reshape(-1)


def solution(mesh):
    placed = (
        P(("grp", "bin", "blk"), None, None, "sub"),
        P(("grp", "bin", "blk"), None, "sub"),
        P(("grp", "bin", "blk"), None),
        P(("grp", "bin", "blk")),
        P(("grp", "bin")),
    )
    return jax.shard_map(
        local,
        mesh=mesh,
        in_specs=placed,
        out_specs=(P(("grp", "bin", "blk")), P(("grp", "bin", "blk"))),
        check_vma=False,
    )
```

```python
import functools

import jax
import jax.numpy as jnp
from jax import lax
from jax.experimental import pallas as pl
from jax.experimental.pallas import tpu as pltpu
from jax.sharding import PartitionSpec as P

MESH = pl.DeviceIdType.MESH
LANES = 128
GROUP = 32


def each(count, body):
    if count <= 16:
        for index in range(count):
            body(index)
    else:
        lax.fori_loop(0, count, lambda index, carry: (body(index), carry)[1], 0)


def landed(window, sem):
    pltpu.make_async_copy(window, window, sem).wait()


def to_column(row):
    parts = []
    for start in range(0, row.shape[1], LANES):
        piece = jnp.broadcast_to(row[:, start:start + LANES], (LANES, LANES))
        parts.append(jnp.transpose(piece))
    return jnp.concatenate(parts, axis=0)


def kernel(owners, blks, reach, slots, valid, masked_hbm, list_hbm, count_hbm, band, far_tiles,
           weight_out, product_out, level_out, masked, far_list, far_count, tiles, column, rows, products, keep_send, keep_all,
           scaled_all, mirror_send, mirror_all, same_send, same_all, cross_send, cross_all,
           pair_send, pair_recv, half_send, half_recv, total_send, total_all, word_sem, load_sem,
           keep_sem, mirror_sem, same_sem, cross_sem, pair_sem, half_sem, total_sem):
    height = column.shape[0]
    count = reach + slots
    device = lax.axis_index("bin") * blks + lax.axis_index("blk")
    side = lax.axis_index("sub")

    def place(owner, core):
        return {"bin": owner // blks, "blk": lax.rem(owner, blks), "sub": core}

    def other(index):
        return lax.rem(device + 1 + index, owners)

    barrier = pltpu.get_barrier_semaphore()

    def greet(index):
        for core in (side, 1 - side):
            pl.semaphore_signal(
                barrier, inc=1, device_id=place(other(index), core), device_id_type=MESH
            )

    each(owners - 1, greet)
    pl.semaphore_signal(barrier, inc=1, device_id=place(device, 1 - side), device_id_type=MESH)

    words = [
        pltpu.make_async_copy(source, target, word_sem.at[at])
        for at, (source, target) in enumerate(
            ((masked_hbm, masked), (list_hbm, far_list), (count_hbm, far_count))
        )
    ]
    for word in words:
        word.start()
    loads = [pltpu.make_async_copy(band.at[0], tiles.at[pl.ds(0, reach)], load_sem.at[0])]
    half_slots = slots // 2
    for piece in range(2):
        loads.append(pltpu.make_async_copy(
            far_tiles.at[pl.ds(piece * half_slots, half_slots)],
            tiles.at[pl.ds(reach + piece * half_slots, half_slots)],
            load_sem.at[1 + piece],
        ))
    for load in loads:
        load.start()
    chunks = [(0, reach), (reach, reach + half_slots), (reach + half_slots, count)]

    keep_all[pl.ds(owners, reach), :] = jnp.zeros((reach, LANES), jnp.float32)
    scaled_all[pl.ds(owners, reach), :] = jnp.zeros((reach, LANES), jnp.float32)
    for step in range(2):
        mirror_all[step, pl.ds(device, 1), :] = jnp.zeros((1, LANES), jnp.float32)

    for word in words:
        word.wait()
    bins = device * height + lax.broadcasted_iota(jnp.int32, (1, height), 1)
    hit = bins == masked[0]
    for index in range(1, masked.shape[0]):
        hit = jnp.logical_or(hit, bins == masked[index])
    keep = jnp.where(hit, 0.0, 1.0).astype(jnp.float32)
    used = [index < far_count[0] for index in range(slots)]

    def send(source, target, sem, owner, core):
        copy = pltpu.make_async_remote_copy(
            src_ref=source,
            dst_ref=target,
            send_sem=sem[0],
            recv_sem=sem[1],
            device_id=place(owner, core),
            device_id_type=MESH,
        )
        copy.start()
        return copy

    def pick(row, core):
        return jnp.where(core == 0, row[:, :LANES], row[:, LANES:])

    def merge(own, across):
        return jnp.concatenate(
            [jnp.where(side == 0, own, across), jnp.where(side == 0, across, own)], axis=1
        )

    mine = pl.ds(device, 1)

    def mirror(step):
        sums = []
        for number, (first, last) in enumerate(chunks):
            if step == 0:
                loads[number].wait()

            def body(index, held):
                window = pl.ds(pl.multiple_of(index * GROUP, GROUP), GROUP)
                own = column[window, :]
                return tuple(
                    old + jnp.sum((tiles[first + at, window, :] * own).reshape(GROUP // 8, 8, LANES), axis=0)
                    for at, old in enumerate(held)
                )

            zero = jnp.zeros((8, LANES), jnp.float32)
            sums.extend(lax.fori_loop(0, height // GROUP, body, (zero,) * (last - first)))
        holder = lax.broadcasted_iota(jnp.int32, (owners, LANES), 0)
        placed = jnp.zeros((owners, LANES), jnp.float32)
        for tile, partial in enumerate(sums):
            if step == 1:
                products[tile] = partial
            if tile == 0:
                continue
            if tile < reach:
                target = device + tile
            else:
                slot = tile - reach
                target = jnp.where(used[slot], far_list[1, slot], -1)
            total = jnp.sum(partial, axis=0, keepdims=True)
            placed = placed + jnp.where(holder == target, total, 0.0)
        mirror_send[step] = placed

        def push(index):
            owner = other(index)
            send(mirror_send.at[step, pl.ds(owner, 1)], mirror_all.at[step, mine],
                 (mirror_sem.at[0, step], mirror_sem.at[1, step]), owner, side)

        each(owners - 1, push)

    def gather(source):
        factors = []
        for tile in range(count):
            if tile < reach:
                factor = source[pl.ds(device + tile, 1), :]
            else:
                slot = tile - reach
                factor = jnp.where(used[slot], source[pl.ds(far_list[1, slot], 1), :], 0.0)
            factors.append(jnp.broadcast_to(factor, (8, LANES)))
        return factors

    def forward(factors):
        def body(index, carry):
            window = pl.ds(pl.multiple_of(index * GROUP, GROUP), GROUP)

            def term(tile):
                return tiles[tile, window, :].reshape(GROUP // 8, 8, LANES) * factors[tile][None]

            whole = term(0)
            for tile in range(1, count):
                whole = whole + term(tile)
            rows[window, :] = whole.reshape(GROUP, LANES)
            return carry

        lax.fori_loop(0, height // GROUP, body, 0)
        pieces = []
        for start in range(0, height, LANES):
            piece = jnp.transpose(rows[pl.ds(start, LANES), :])
            pieces.append(jnp.sum(piece, axis=0, keepdims=True))
        return jnp.concatenate(pieces, axis=1)

    def mirrored(step):
        landed(mirror_all.at[step, pl.ds(0, owners - 1)], mirror_sem.at[1, step])
        return jnp.sum(mirror_all[step], axis=0, keepdims=True)

    keep_half = pick(keep, side)
    keep_send[...] = keep_half
    keep_all[mine, :] = keep_half
    column[...] = to_column(keep)
    pl.semaphore_wait(barrier, 2 * owners - 1)
    each(owners - 1, lambda index: send(
        keep_send, keep_all.at[mine], (keep_sem.at[0], keep_sem.at[1]), other(index), side))
    mirror(0)
    landed(keep_all.at[pl.ds(0, owners - 1)], keep_sem.at[1])
    row_part = forward(gather(keep_all))
    same = pick(row_part, side) + mirrored(0)
    cross = pick(row_part, 1 - side)
    same_send[...] = same
    same_all[mine, :] = same
    cross_send[...] = cross
    pair_send[...] = jnp.concatenate([cross, same], axis=0)

    def spread(index):
        owner = other(index)
        send(same_send, same_all.at[mine], (same_sem.at[0], same_sem.at[1]), owner, side)
        send(cross_send, cross_all.at[mine], (cross_sem.at[0], cross_sem.at[1]), owner, 1 - side)

    each(owners - 1, spread)
    pair = send(pair_send, pair_recv, (pair_sem.at[0], pair_sem.at[1]), device, 1 - side)
    pair.wait_recv()
    across = pair_recv[0:1, :]
    cross_all[mine, :] = across
    sums = merge(same + across, cross + pair_recv[1:2, :])
    scaled = keep / jnp.sqrt(sums)
    column[...] = to_column(scaled)
    mirror(1)
    landed(same_all.at[pl.ds(0, owners - 1)], same_sem.at[1])
    landed(cross_all.at[pl.ds(0, owners - 1)], cross_sem.at[1])
    scaled_all[pl.ds(0, owners), :] = keep_all[pl.ds(0, owners), :] / jnp.sqrt(same_all[...] + cross_all[...])
    factors = gather(scaled_all)
    form = products[1] * factors[1]
    for tile in range(2, count):
        form = form + products[tile] * factors[tile]
    form = jnp.sum(products[0] * factors[0] + 2.0 * form, axis=0, keepdims=True)
    packet = jnp.concatenate([pick(keep * sums, side), form], axis=0)
    total_send[...] = packet
    slot = device * 2 + side
    total_all[slot] = packet
    pair_total = (total_sem.at[0], total_sem.at[1])

    def announce(index):
        for core in (side, 1 - side):
            send(total_send, total_all.at[slot], pair_total, other(index), core)

    each(owners - 1, announce)
    send(total_send, total_all.at[slot], pair_total, device, 1 - side)

    row_part = forward(factors)
    col_half = mirrored(1)
    part = row_part + merge(col_half, jnp.zeros_like(col_half))
    half_send[...] = part
    half = send(half_send, half_recv, (half_sem.at[0], half_sem.at[1]), device, 1 - side)
    half.wait_recv()
    product = part + half_recv[...]
    landed(total_all.at[pl.ds(0, 2 * owners - 1)], total_sem.at[1])
    totals = jnp.sum(jnp.sum(total_all[...], axis=0), axis=1, keepdims=True) / valid
    first = totals[0:1]
    mean = first * totals[1:2]
    weight_out[...] = scaled * first
    product_out[...] = product
    level_out[...] = scaled * mean

    landed(keep_all.at[pl.ds(0, owners - 1)], keep_sem.at[0])
    landed(same_all.at[pl.ds(0, owners - 1)], same_sem.at[0])
    landed(cross_all.at[pl.ds(0, owners - 1)], cross_sem.at[0])
    pair.wait_send()
    half.wait_send()
    for step in range(2):
        landed(mirror_all.at[step, pl.ds(0, owners - 1)], mirror_sem.at[0, step])
    landed(total_all.at[pl.ds(0, 2 * owners - 1)], total_sem.at[0])


def local(band, far_tiles, far_list, far_count, masked):
    reach, block, half = band.shape[1:]
    slots = far_tiles.shape[0]
    owners = lax.axis_size(("bin", "blk"))
    valid = owners * block - lax.axis_size("bin") * masked.shape[0]
    hbm = pl.BlockSpec(memory_space=pl.ANY)
    vmem = pl.BlockSpec(memory_space=pltpu.VMEM)
    f32 = jnp.float32
    dma = pltpu.SemaphoreType.DMA
    weight, product, level = pl.pallas_call(
        functools.partial(kernel, owners, lax.axis_size("blk"), reach, slots, float(valid)),
        out_shape=(jax.ShapeDtypeStruct((1, block), f32),) * 3,
        out_specs=(vmem,) * 3,
        in_specs=[hbm] * 5,
        scratch_shapes=[
            pltpu.SMEM(masked.shape, jnp.int32),
            pltpu.SMEM((2, slots), jnp.int32),
            pltpu.SMEM((1,), jnp.int32),
            pltpu.VMEM((reach + slots, block, half), f32),
            pltpu.VMEM((block, half), f32),
            pltpu.VMEM((block, half), f32),
            pltpu.VMEM((reach + slots, 8, half), f32),
            pltpu.VMEM((1, half), f32),
            pltpu.VMEM((owners + reach, half), f32),
            pltpu.VMEM((owners + reach, half), f32),
            pltpu.VMEM((2, owners, half), f32),
            pltpu.VMEM((2, owners, half), f32),
            pltpu.VMEM((1, half), f32),
            pltpu.VMEM((owners, half), f32),
            pltpu.VMEM((1, half), f32),
            pltpu.VMEM((owners, half), f32),
            pltpu.VMEM((2, half), f32),
            pltpu.VMEM((2, half), f32),
            pltpu.VMEM((1, block), f32),
            pltpu.VMEM((1, block), f32),
            pltpu.VMEM((2, half), f32),
            pltpu.VMEM((2 * owners, 2, half), f32),
            dma((3,)),
            dma((3,)),
            dma((2,)),
            dma((2, 2)),
            dma((2,)),
            dma((2,)),
            dma((2,)),
            dma((2,)),
            dma((2,)),
        ],
        compiler_params=pltpu.CompilerParams(collective_id=0, has_side_effects=True),
    )(masked, far_list.T, far_count, band, far_tiles)
    weight, product, level = weight.reshape(-1), product.reshape(-1), level.reshape(-1)
    return jnp.sqrt(level / product), weight * product


def solution(mesh):
    placed = (
        P(("grp", "bin", "blk"), None, None, "sub"),
        P(("grp", "bin", "blk"), None, "sub"),
        P(("grp", "bin", "blk"), None),
        P(("grp", "bin", "blk")),
        P(("grp", "bin")),
    )
    return jax.shard_map(
        local,
        mesh=mesh,
        in_specs=placed,
        out_specs=(P(("grp", "bin", "blk")), P(("grp", "bin", "blk"))),
        check_vma=False,
    )
```

```python
import functools

import jax
import jax.numpy as jnp
from jax import lax
from jax.experimental import pallas as pl
from jax.experimental.pallas import tpu as pltpu
from jax.sharding import PartitionSpec as P

MESH = pl.DeviceIdType.MESH
LANES = 128
PIECE = 2
GROUP = 32


def each(count, body):
    if count <= 16:
        for index in range(count):
            body(index)
    else:
        lax.fori_loop(0, count, lambda index, carry: (body(index), carry)[1], 0)


def landed(window, sem):
    pltpu.make_async_copy(window, window, sem).wait()


def to_column(row):
    parts = []
    for start in range(0, row.shape[1], LANES):
        piece = jnp.broadcast_to(row[:, start:start + LANES], (LANES, LANES))
        parts.append(jnp.transpose(piece))
    return jnp.concatenate(parts, axis=0)


def kernel(owners, blks, reach, slots, valid, masked_hbm, list_hbm, count_hbm, band, far_tiles,
           weight_out, product_out, level_out, masked, far_list, far_count, tiles, column, rows, products, keep_send, keep_all,
           scaled_all, mirror_send, mirror_all, same_send, same_all, cross_send, cross_all,
           pair_send, pair_recv, half_send, half_recv, total_send, total_all, word_sem, load_sem,
           keep_sem, mirror_sem, same_sem, cross_sem, pair_sem, half_sem, total_sem):
    height = column.shape[0]
    count = reach + slots
    device = lax.axis_index("bin") * blks + lax.axis_index("blk")
    side = lax.axis_index("sub")

    def place(owner, core):
        return {"bin": owner // blks, "blk": lax.rem(owner, blks), "sub": core}

    def other(index):
        return lax.rem(device + 1 + index, owners)

    barrier = pltpu.get_barrier_semaphore()

    def greet(index):
        for core in (side, 1 - side):
            pl.semaphore_signal(
                barrier, inc=1, device_id=place(other(index), core), device_id_type=MESH
            )


    words = [
        pltpu.make_async_copy(source, target, word_sem.at[at])
        for at, (source, target) in enumerate(
            ((masked_hbm, masked), (list_hbm, far_list), (count_hbm, far_count))
        )
    ]
    for word in words:
        word.start()
    half_slots = slots // 2
    chunks = [(0, reach), (reach, reach + half_slots), (reach + half_slots, count)]
    for number, (first, last) in enumerate(chunks):
        source = band.at[0] if number == 0 else far_tiles
        skip = 0 if number == 0 else reach
        for at in range(first, last, PIECE):
            pltpu.make_async_copy(
                source.at[pl.ds(at - skip, PIECE)], tiles.at[pl.ds(at, PIECE)], load_sem.at[number]
            ).start()

    each(owners - 1, greet)
    pl.semaphore_signal(barrier, inc=1, device_id=place(device, 1 - side), device_id_type=MESH)

    keep_all[pl.ds(owners, reach), :] = jnp.zeros((reach, LANES), jnp.float32)
    scaled_all[pl.ds(owners, reach), :] = jnp.zeros((reach, LANES), jnp.float32)
    for step in range(2):
        mirror_all[step, pl.ds(device, 1), :] = jnp.zeros((1, LANES), jnp.float32)

    for word in words:
        word.wait()
    bins = device * height + lax.broadcasted_iota(jnp.int32, (1, height), 1)
    hit = bins == masked[0]
    for index in range(1, masked.shape[0]):
        hit = jnp.logical_or(hit, bins == masked[index])
    keep = jnp.where(hit, 0.0, 1.0).astype(jnp.float32)
    used = [index < far_count[0] for index in range(slots)]

    def send(source, target, sem, owner, core):
        copy = pltpu.make_async_remote_copy(
            src_ref=source,
            dst_ref=target,
            send_sem=sem[0],
            recv_sem=sem[1],
            device_id=place(owner, core),
            device_id_type=MESH,
        )
        copy.start()
        return copy

    def pick(row, core):
        return jnp.where(core == 0, row[:, :LANES], row[:, LANES:])

    def merge(own, across):
        return jnp.concatenate(
            [jnp.where(side == 0, own, across), jnp.where(side == 0, across, own)], axis=1
        )

    mine = pl.ds(device, 1)

    def mirror(step):
        sums = []
        for number, (first, last) in enumerate(chunks):
            if step == 0:
                landed(tiles.at[pl.ds(first, last - first)], load_sem.at[number])

            def body(index, held):
                window = pl.ds(pl.multiple_of(index * GROUP, GROUP), GROUP)
                own = column[window, :]
                return tuple(
                    old + jnp.sum((tiles[first + at, window, :] * own).reshape(GROUP // 8, 8, LANES), axis=0)
                    for at, old in enumerate(held)
                )

            zero = jnp.zeros((8, LANES), jnp.float32)
            sums.extend(lax.fori_loop(0, height // GROUP, body, (zero,) * (last - first)))
        holder = lax.broadcasted_iota(jnp.int32, (owners, LANES), 0)
        placed = jnp.zeros((owners, LANES), jnp.float32)
        for tile, partial in enumerate(sums):
            if step == 1:
                products[tile] = partial
            if tile == 0:
                continue
            if tile < reach:
                target = device + tile
            else:
                slot = tile - reach
                target = jnp.where(used[slot], far_list[1, slot], -1)
            total = jnp.sum(partial, axis=0, keepdims=True)
            placed = placed + jnp.where(holder == target, total, 0.0)
        mirror_send[step] = placed

        def push(index):
            owner = other(index)
            send(mirror_send.at[step, pl.ds(owner, 1)], mirror_all.at[step, mine],
                 (mirror_sem.at[0, step], mirror_sem.at[1, step]), owner, side)

        each(owners - 1, push)

    def gather(source):
        factors = []
        for tile in range(count):
            if tile < reach:
                factor = source[pl.ds(device + tile, 1), :]
            else:
                slot = tile - reach
                factor = jnp.where(used[slot], source[pl.ds(far_list[1, slot], 1), :], 0.0)
            factors.append(jnp.broadcast_to(factor, (8, LANES)))
        return factors

    def forward(factors):
        pieces = []
        for start in range(0, height, LANES):
            for at in range(start, start + LANES, GROUP):
                window = pl.ds(at, GROUP)

                def term(tile):
                    return tiles[tile, window, :].reshape(GROUP // 8, 8, LANES) * factors[tile][None]

                whole = term(0)
                for tile in range(1, count):
                    whole = whole + term(tile)
                rows[window, :] = whole.reshape(GROUP, LANES)
            piece = jnp.transpose(rows[pl.ds(start, LANES), :])
            pieces.append(jnp.sum(piece, axis=0, keepdims=True))
        return jnp.concatenate(pieces, axis=1)

    def mirrored(step):
        landed(mirror_all.at[step, pl.ds(0, owners - 1)], mirror_sem.at[1, step])
        return jnp.sum(mirror_all[step], axis=0, keepdims=True)

    keep_half = pick(keep, side)
    keep_send[...] = keep_half
    keep_all[mine, :] = keep_half
    column[...] = to_column(keep)
    pl.semaphore_wait(barrier, 2 * owners - 1)
    each(owners - 1, lambda index: send(
        keep_send, keep_all.at[mine], (keep_sem.at[0], keep_sem.at[1]), other(index), side))
    mirror(0)
    landed(keep_all.at[pl.ds(0, owners - 1)], keep_sem.at[1])
    row_part = forward(gather(keep_all))
    same = pick(row_part, side) + mirrored(0)
    cross = pick(row_part, 1 - side)
    same_send[...] = same
    same_all[mine, :] = same
    cross_send[...] = cross
    pair_send[...] = jnp.concatenate([cross, same], axis=0)

    def spread(index):
        owner = other(index)
        send(same_send, same_all.at[mine], (same_sem.at[0], same_sem.at[1]), owner, side)
        send(cross_send, cross_all.at[mine], (cross_sem.at[0], cross_sem.at[1]), owner, 1 - side)

    each(owners - 1, spread)
    pair = send(pair_send, pair_recv, (pair_sem.at[0], pair_sem.at[1]), device, 1 - side)
    pair.wait_recv()
    across = pair_recv[0:1, :]
    cross_all[mine, :] = across
    sums = merge(same + across, cross + pair_recv[1:2, :])
    scaled = keep / jnp.sqrt(sums)
    column[...] = to_column(scaled)
    mirror(1)
    landed(same_all.at[pl.ds(0, owners - 1)], same_sem.at[1])
    landed(cross_all.at[pl.ds(0, owners - 1)], cross_sem.at[1])
    scaled_all[pl.ds(0, owners), :] = keep_all[pl.ds(0, owners), :] / jnp.sqrt(same_all[...] + cross_all[...])
    factors = gather(scaled_all)
    form = products[1] * factors[1]
    for tile in range(2, count):
        form = form + products[tile] * factors[tile]
    form = jnp.sum(products[0] * factors[0] + 2.0 * form, axis=0, keepdims=True)
    packet = jnp.concatenate([pick(keep * sums, side), form], axis=0)
    total_send[...] = packet
    slot = device * 2 + side
    total_all[slot] = packet
    pair_total = (total_sem.at[0], total_sem.at[1])

    def announce(index):
        for core in (side, 1 - side):
            send(total_send, total_all.at[slot], pair_total, other(index), core)

    each(owners - 1, announce)
    send(total_send, total_all.at[slot], pair_total, device, 1 - side)

    row_part = forward(factors)
    col_half = mirrored(1)
    part = row_part + merge(col_half, jnp.zeros_like(col_half))
    half_send[...] = part
    half = send(half_send, half_recv, (half_sem.at[0], half_sem.at[1]), device, 1 - side)
    half.wait_recv()
    product = part + half_recv[...]
    landed(total_all.at[pl.ds(0, 2 * owners - 1)], total_sem.at[1])
    totals = jnp.sum(jnp.sum(total_all[...], axis=0), axis=1, keepdims=True) / valid
    first = totals[0:1]
    mean = first * totals[1:2]
    weight_out[...] = scaled * first
    product_out[...] = product
    level_out[...] = scaled * mean

    landed(keep_all.at[pl.ds(0, owners - 1)], keep_sem.at[0])
    landed(same_all.at[pl.ds(0, owners - 1)], same_sem.at[0])
    landed(cross_all.at[pl.ds(0, owners - 1)], cross_sem.at[0])
    pair.wait_send()
    half.wait_send()
    for step in range(2):
        landed(mirror_all.at[step, pl.ds(0, owners - 1)], mirror_sem.at[0, step])
    landed(total_all.at[pl.ds(0, 2 * owners - 1)], total_sem.at[0])


def local(band, far_tiles, far_list, far_count, masked):
    reach, block, half = band.shape[1:]
    slots = far_tiles.shape[0]
    owners = lax.axis_size(("bin", "blk"))
    valid = owners * block - lax.axis_size("bin") * masked.shape[0]
    hbm = pl.BlockSpec(memory_space=pl.ANY)
    vmem = pl.BlockSpec(memory_space=pltpu.VMEM)
    f32 = jnp.float32
    dma = pltpu.SemaphoreType.DMA
    weight, product, level = pl.pallas_call(
        functools.partial(kernel, owners, lax.axis_size("blk"), reach, slots, float(valid)),
        out_shape=(jax.ShapeDtypeStruct((1, block), f32),) * 3,
        out_specs=(vmem,) * 3,
        in_specs=[hbm] * 5,
        scratch_shapes=[
            pltpu.SMEM(masked.shape, jnp.int32),
            pltpu.SMEM((2, slots), jnp.int32),
            pltpu.SMEM((1,), jnp.int32),
            pltpu.VMEM((reach + slots, block, half), f32),
            pltpu.VMEM((block, half), f32),
            pltpu.VMEM((block, half), f32),
            pltpu.VMEM((reach + slots, 8, half), f32),
            pltpu.VMEM((1, half), f32),
            pltpu.VMEM((owners + reach, half), f32),
            pltpu.VMEM((owners + reach, half), f32),
            pltpu.VMEM((2, owners, half), f32),
            pltpu.VMEM((2, owners, half), f32),
            pltpu.VMEM((1, half), f32),
            pltpu.VMEM((owners, half), f32),
            pltpu.VMEM((1, half), f32),
            pltpu.VMEM((owners, half), f32),
            pltpu.VMEM((2, half), f32),
            pltpu.VMEM((2, half), f32),
            pltpu.VMEM((1, block), f32),
            pltpu.VMEM((1, block), f32),
            pltpu.VMEM((2, half), f32),
            pltpu.VMEM((2 * owners, 2, half), f32),
            dma((3,)),
            dma((3,)),
            dma((2,)),
            dma((2, 2)),
            dma((2,)),
            dma((2,)),
            dma((2,)),
            dma((2,)),
            dma((2,)),
        ],
        compiler_params=pltpu.CompilerParams(collective_id=0, has_side_effects=True),
    )(masked, far_list.T, far_count, band, far_tiles)
    weight, product, level = weight.reshape(-1), product.reshape(-1), level.reshape(-1)
    return jnp.sqrt(level / product), weight * product


def solution(mesh):
    placed = (
        P(("grp", "bin", "blk"), None, None, "sub"),
        P(("grp", "bin", "blk"), None, "sub"),
        P(("grp", "bin", "blk"), None),
        P(("grp", "bin", "blk")),
        P(("grp", "bin")),
    )
    return jax.shard_map(
        local,
        mesh=mesh,
        in_specs=placed,
        out_specs=(P(("grp", "bin", "blk")), P(("grp", "bin", "blk"))),
        check_vma=False,
    )
```

```python
import functools

import jax
import jax.numpy as jnp
from jax import lax
from jax.experimental import pallas as pl
from jax.experimental.pallas import tpu as pltpu
from jax.sharding import PartitionSpec as P

MESH = pl.DeviceIdType.MESH
LANES = 128
PIECE = 2
GROUP = 32


def each(count, body):
    if count <= 16:
        for index in range(count):
            body(index)
    else:
        lax.fori_loop(0, count, lambda index, carry: (body(index), carry)[1], 0)


def landed(window, sem):
    pltpu.make_async_copy(window, window, sem).wait()


def to_column(row):
    parts = []
    for start in range(0, row.shape[1], LANES):
        piece = jnp.broadcast_to(row[:, start:start + LANES], (LANES, LANES))
        parts.append(jnp.transpose(piece))
    return jnp.concatenate(parts, axis=0)


def kernel(owners, blks, reach, slots, valid, masked_hbm, list_hbm, far_count, band, far_tiles,
           weight_out, product_out, level_out, masked, far_list, tiles, column, rows, products, keep_send, keep_all,
           scaled_all, mirror_send, mirror_all, same_send, same_all, cross_send, cross_all,
           pair_send, pair_recv, half_send, half_recv, total_send, total_all, word_sem, load_sem,
           keep_sem, mirror_sem, same_sem, cross_sem, pair_sem, half_sem, total_sem):
    height = column.shape[0]
    count = reach + slots
    device = lax.axis_index("bin") * blks + lax.axis_index("blk")
    side = lax.axis_index("sub")

    def place(owner, core):
        return {"bin": owner // blks, "blk": lax.rem(owner, blks), "sub": core}

    def other(index):
        return lax.rem(device + 1 + index, owners)

    barrier = pltpu.get_barrier_semaphore()

    def greet(index):
        for core in (side, 1 - side):
            pl.semaphore_signal(
                barrier, inc=1, device_id=place(other(index), core), device_id_type=MESH
            )


    words = [
        pltpu.make_async_copy(source, target, word_sem.at[at])
        for at, (source, target) in enumerate(
            ((masked_hbm, masked), (list_hbm, far_list))
        )
    ]
    for word in words:
        word.start()
    half_slots = slots // 2
    chunks = [(0, reach), (reach, reach + half_slots), (reach + half_slots, count)]
    for number, (first, last) in enumerate(chunks):
        source = band.at[0] if number == 0 else far_tiles
        skip = 0 if number == 0 else reach
        for at in range(first, last, PIECE):
            pltpu.make_async_copy(
                source.at[pl.ds(at - skip, PIECE)], tiles.at[pl.ds(at, PIECE)], load_sem.at[number]
            ).start()

    each(owners - 1, greet)
    pl.semaphore_signal(barrier, inc=1, device_id=place(device, 1 - side), device_id_type=MESH)

    keep_all[pl.ds(owners, reach), :] = jnp.zeros((reach, LANES), jnp.float32)
    scaled_all[pl.ds(owners, reach), :] = jnp.zeros((reach, LANES), jnp.float32)
    for step in range(2):
        mirror_all[step, pl.ds(device, 1), :] = jnp.zeros((1, LANES), jnp.float32)

    for word in words:
        word.wait()
    bins = device * height + lax.broadcasted_iota(jnp.int32, (1, height), 1)
    hit = bins == masked[0]
    for index in range(1, masked.shape[0]):
        hit = jnp.logical_or(hit, bins == masked[index])
    keep = jnp.where(hit, 0.0, 1.0).astype(jnp.float32)
    used = [index < far_count[0] for index in range(slots)]

    def send(source, target, sem, owner, core):
        copy = pltpu.make_async_remote_copy(
            src_ref=source,
            dst_ref=target,
            send_sem=sem[0],
            recv_sem=sem[1],
            device_id=place(owner, core),
            device_id_type=MESH,
        )
        copy.start()
        return copy

    def pick(row, core):
        return jnp.where(core == 0, row[:, :LANES], row[:, LANES:])

    def merge(own, across):
        return jnp.concatenate(
            [jnp.where(side == 0, own, across), jnp.where(side == 0, across, own)], axis=1
        )

    mine = pl.ds(device, 1)

    def mirror(step):
        sums = []
        for number, (first, last) in enumerate(chunks):
            if step == 0:
                landed(tiles.at[pl.ds(first, last - first)], load_sem.at[number])

            def body(index, held):
                window = pl.ds(pl.multiple_of(index * GROUP, GROUP), GROUP)
                own = column[window, :]
                return tuple(
                    old + jnp.sum((tiles[first + at, window, :] * own).reshape(GROUP // 8, 8, LANES), axis=0)
                    for at, old in enumerate(held)
                )

            zero = jnp.zeros((8, LANES), jnp.float32)
            sums.extend(lax.fori_loop(0, height // GROUP, body, (zero,) * (last - first)))
        holder = lax.broadcasted_iota(jnp.int32, (owners, LANES), 0)
        placed = jnp.zeros((owners, LANES), jnp.float32)
        for tile, partial in enumerate(sums):
            if step == 1:
                products[tile] = partial
            if tile == 0:
                continue
            if tile < reach:
                target = device + tile
            else:
                slot = tile - reach
                target = jnp.where(used[slot], far_list[1, slot], -1)
            total = jnp.sum(partial, axis=0, keepdims=True)
            placed = placed + jnp.where(holder == target, total, 0.0)
        mirror_send[step] = placed

        def push(index):
            owner = other(index)
            send(mirror_send.at[step, pl.ds(owner, 1)], mirror_all.at[step, mine],
                 (mirror_sem.at[0, step], mirror_sem.at[1, step]), owner, side)

        each(owners - 1, push)

    def gather(source):
        factors = []
        for tile in range(count):
            if tile < reach:
                factor = source[pl.ds(device + tile, 1), :]
            else:
                slot = tile - reach
                factor = jnp.where(used[slot], source[pl.ds(far_list[1, slot], 1), :], 0.0)
            factors.append(jnp.broadcast_to(factor, (8, LANES)))
        return factors

    def forward(factors):
        pieces = []
        for start in range(0, height, LANES):
            for at in range(start, start + LANES, GROUP):
                window = pl.ds(at, GROUP)

                def term(tile):
                    return tiles[tile, window, :].reshape(GROUP // 8, 8, LANES) * factors[tile][None]

                whole = term(0)
                for tile in range(1, count):
                    whole = whole + term(tile)
                rows[window, :] = whole.reshape(GROUP, LANES)
            piece = jnp.transpose(rows[pl.ds(start, LANES), :])
            pieces.append(jnp.sum(piece, axis=0, keepdims=True))
        return jnp.concatenate(pieces, axis=1)

    def mirrored(step):
        landed(mirror_all.at[step, pl.ds(0, owners - 1)], mirror_sem.at[1, step])
        return jnp.sum(mirror_all[step], axis=0, keepdims=True)

    keep_half = pick(keep, side)
    keep_send[...] = keep_half
    keep_all[mine, :] = keep_half
    column[...] = to_column(keep)
    pl.semaphore_wait(barrier, 2 * owners - 1)
    each(owners - 1, lambda index: send(
        keep_send, keep_all.at[mine], (keep_sem.at[0], keep_sem.at[1]), other(index), side))
    mirror(0)
    landed(keep_all.at[pl.ds(0, owners - 1)], keep_sem.at[1])
    row_part = forward(gather(keep_all))
    same = pick(row_part, side) + mirrored(0)
    cross = pick(row_part, 1 - side)
    same_send[...] = same
    same_all[mine, :] = same
    cross_send[...] = cross
    pair_send[...] = jnp.concatenate([cross, same], axis=0)

    def spread(index):
        owner = other(index)
        send(same_send, same_all.at[mine], (same_sem.at[0], same_sem.at[1]), owner, side)
        send(cross_send, cross_all.at[mine], (cross_sem.at[0], cross_sem.at[1]), owner, 1 - side)

    each(owners - 1, spread)
    pair = send(pair_send, pair_recv, (pair_sem.at[0], pair_sem.at[1]), device, 1 - side)
    pair.wait_recv()
    across = pair_recv[0:1, :]
    cross_all[mine, :] = across
    sums = merge(same + across, cross + pair_recv[1:2, :])
    scaled = keep * lax.rsqrt(sums)
    column[...] = to_column(scaled)
    mirror(1)
    landed(same_all.at[pl.ds(0, owners - 1)], same_sem.at[1])
    landed(cross_all.at[pl.ds(0, owners - 1)], cross_sem.at[1])
    scaled_all[pl.ds(0, owners), :] = keep_all[pl.ds(0, owners), :] * lax.rsqrt(same_all[...] + cross_all[...])
    factors = gather(scaled_all)
    form = products[1] * factors[1]
    for tile in range(2, count):
        form = form + products[tile] * factors[tile]
    form = jnp.sum(products[0] * factors[0] + 2.0 * form, axis=0, keepdims=True)
    packet = jnp.concatenate([pick(keep * sums, side), form], axis=0)
    total_send[...] = packet
    slot = device * 2 + side
    total_all[slot] = packet
    pair_total = (total_sem.at[0], total_sem.at[1])

    def announce(index):
        for core in (side, 1 - side):
            send(total_send, total_all.at[slot], pair_total, other(index), core)

    each(owners - 1, announce)
    send(total_send, total_all.at[slot], pair_total, device, 1 - side)

    row_part = forward(factors)
    col_half = mirrored(1)
    part = row_part + merge(col_half, jnp.zeros_like(col_half))
    half_send[...] = part
    half = send(half_send, half_recv, (half_sem.at[0], half_sem.at[1]), device, 1 - side)
    half.wait_recv()
    product = part + half_recv[...]
    landed(total_all.at[pl.ds(0, 2 * owners - 1)], total_sem.at[1])
    totals = jnp.sum(jnp.sum(total_all[...], axis=0), axis=1, keepdims=True) / valid
    first = totals[0:1]
    mean = first * totals[1:2]
    weight_out[...] = scaled * first
    product_out[...] = product
    level_out[...] = scaled * mean

    landed(keep_all.at[pl.ds(0, owners - 1)], keep_sem.at[0])
    landed(same_all.at[pl.ds(0, owners - 1)], same_sem.at[0])
    landed(cross_all.at[pl.ds(0, owners - 1)], cross_sem.at[0])
    pair.wait_send()
    half.wait_send()
    for step in range(2):
        landed(mirror_all.at[step, pl.ds(0, owners - 1)], mirror_sem.at[0, step])
    landed(total_all.at[pl.ds(0, 2 * owners - 1)], total_sem.at[0])


def local(band, far_tiles, far_list, far_count, masked):
    reach, block, half = band.shape[1:]
    slots = far_tiles.shape[0]
    owners = lax.axis_size(("bin", "blk"))
    valid = owners * block - lax.axis_size("bin") * masked.shape[0]
    hbm = pl.BlockSpec(memory_space=pl.ANY)
    vmem = pl.BlockSpec(memory_space=pltpu.VMEM)
    f32 = jnp.float32
    dma = pltpu.SemaphoreType.DMA
    weight, product, level = pl.pallas_call(
        functools.partial(kernel, owners, lax.axis_size("blk"), reach, slots, float(valid)),
        out_shape=(jax.ShapeDtypeStruct((1, block), f32),) * 3,
        out_specs=(vmem,) * 3,
        in_specs=[hbm, hbm, pl.BlockSpec(memory_space=pltpu.SMEM), hbm, hbm],
        scratch_shapes=[
            pltpu.SMEM(masked.shape, jnp.int32),
            pltpu.SMEM((2, slots), jnp.int32),
            pltpu.VMEM((reach + slots, block, half), f32),
            pltpu.VMEM((block, half), f32),
            pltpu.VMEM((block, half), f32),
            pltpu.VMEM((reach + slots, 8, half), f32),
            pltpu.VMEM((1, half), f32),
            pltpu.VMEM((owners + reach, half), f32),
            pltpu.VMEM((owners + reach, half), f32),
            pltpu.VMEM((2, owners, half), f32),
            pltpu.VMEM((2, owners, half), f32),
            pltpu.VMEM((1, half), f32),
            pltpu.VMEM((owners, half), f32),
            pltpu.VMEM((1, half), f32),
            pltpu.VMEM((owners, half), f32),
            pltpu.VMEM((2, half), f32),
            pltpu.VMEM((2, half), f32),
            pltpu.VMEM((1, block), f32),
            pltpu.VMEM((1, block), f32),
            pltpu.VMEM((2, half), f32),
            pltpu.VMEM((2 * owners, 2, half), f32),
            dma((2,)),
            dma((3,)),
            dma((2,)),
            dma((2, 2)),
            dma((2,)),
            dma((2,)),
            dma((2,)),
            dma((2,)),
            dma((2,)),
        ],
        compiler_params=pltpu.CompilerParams(collective_id=0, has_side_effects=True),
    )(masked, far_list.T, far_count, band, far_tiles)
    weight, product, level = weight.reshape(-1), product.reshape(-1), level.reshape(-1)
    return jnp.sqrt(level / product), weight * product


def solution(mesh):
    placed = (
        P(("grp", "bin", "blk"), None, None, "sub"),
        P(("grp", "bin", "blk"), None, "sub"),
        P(("grp", "bin", "blk"), None),
        P(("grp", "bin", "blk")),
        P(("grp", "bin")),
    )
    return jax.shard_map(
        local,
        mesh=mesh,
        in_specs=placed,
        out_specs=(P(("grp", "bin", "blk")), P(("grp", "bin", "blk"))),
        check_vma=False,
    )
```
